32 devices in a mesh: dp: 8 (over z, y), tensor: 4 (over x, core).
Axes of the slice: x: 2, y: 2, z: 4, core: 2. Of those that a mesh axis runs over, the one named last changes fastest.
Arguments:
- hidden: float32 [12288, 768], P(('dp', 'tensor')), may hold values from -6 to 6
- segments: int32 [12288], P('dp'), may hold values from 0 to 512, as said below
- w_qkv: bfloat16 [2, 768, 2304], P(None, 'dp', 'tensor'), may hold values from -0.21875 to 0.21875
- w_out: bfloat16 [2, 768, 768], P(None, 'dp', 'tensor'), may hold values from -0.875 to 0.875
- w_up: bfloat16 [2, 768, 3072], P(None, 'dp', 'tensor'), may hold values from -0.21875 to 0.21875
- w_down: bfloat16 [2, 768, 3072], P(None, 'dp', 'tensor'), may hold values from -0.109375 to 0.109375
- ln_gain: float32 [2, 2, 768], replicated, may hold values from 0.5 to 1.5
- ln_bias: float32 [2, 2, 768], replicated, may hold values from -1.8 to 1.8
- branch_bias: float32 [2, 768], replicated, may hold values from -1.8 to 1.8
- qkv_bias: float32 [2, 2304], replicated, may hold values from -1.8 to 1.8
- up_bias: float32 [2, 3072], replicated, may hold values from -1.8 to 1.8
- cotangent: float32 [12288, 768], P(('dp', 'tensor')), may hold values from -6 to 6
Outputs:
- hidden_out: float32 [12288, 768], P(('dp', 'tensor'))
- hidden_grad: float32 [12288, 768], P(('dp', 'tensor'))
- w_qkv_grad: float32 [2, 768, 2304], P(None, 'dp', 'tensor')
- w_out_grad: float32 [2, 768, 768], P(None, 'dp', 'tensor')
- w_up_grad: float32 [2, 768, 3072], P(None, 'dp', 'tensor')
- w_down_grad: float32 [2, 768, 3072], P(None, 'dp', 'tensor')
- ln_gain_grad: float32 [2, 2, 768], replicated
- ln_bias_grad: float32 [2, 2, 768], replicated
- branch_bias_grad: float32 [2, 768], replicated
- qkv_bias_grad: float32 [2, 2304], replicated
- up_bias_grad: float32 [2, 3072], replicated
The draws below stay inside these ranges and needn't reach their ends.
Inputs may be any that keep to these rules, and one draw needn't show every extreme that they name: `segments`: within each group of 1536 consecutive tokens the ids start at 0 and rise by one where a new sequence begins; every sequence has at most 1024 tokens, and each group holds one of exactly 1024.
All inputs are finite; a program needn't handle non-finite values.
Results may differ from the reference program's by a relative error of at most 0.018.
Values may be sent and summed in bfloat16 or wider, within the bound.
A program may use at most 192 MiB of HBM per device.

```python
import math
import jax
import jax.numpy as jnp
from jax import lax

D = 768
HEADS = 12
HEAD_DIM = 64
FF = 3072
ROT = 16
LAYERS = 2
GROUP_TOK = 1536
TOKENS = 12288
LONGEST = 1024


def draw_segments(key, part):
    key = jax.random.fold_in(key, 11)
    group_count = TOKENS // GROUP_TOK
    start_key, rate_key, cut_key, full_key = jax.random.split(key, 4)
    long_start = jax.random.randint(start_key, (group_count, 1), 0, GROUP_TOK - LONGEST + 1)
    rate_level = jax.random.randint(rate_key, (group_count, 1), 0, 4)
    full_group = jax.random.randint(full_key, (), 0, group_count)
    group_ids = jnp.arange(group_count, dtype=jnp.int32)[:, None]
    places = jnp.arange(GROUP_TOK, dtype=jnp.int32)[None, :]
    dice = jax.random.randint(cut_key, (group_count, GROUP_TOK), 0, 256)
    limit = jnp.where(rate_level == 0, 0, jnp.power(2, rate_level + 1))
    limit = jnp.where(group_ids == full_group, 256, limit)
    inside = (places > long_start) & (places < long_start + LONGEST)
    forced = (places == 0) | (places == long_start) | (places == long_start + LONGEST) | (places % LONGEST == 0)
    cuts = ((dice < limit) | forced) & jnp.logical_not(inside)
    return (jnp.cumsum(cuts.astype(jnp.int32), axis=1) - 1).astype(jnp.int32).reshape(TOKENS)


def with_spikes(entries, stream_key, source, target, blocks, factor):
    owner, partner = [(jnp.arange(entries.shape[position]) // (entries.shape[position] // blocks)).reshape([-1 if axis == position else 1 for axis in range(entries.ndim)]) for position in (source, target)]
    chosen = jax.random.permutation(stream_key, blocks)[partner]
    strong = (owner == chosen) | (owner == (partner + blocks // 2) % blocks)
    return jnp.where(strong, factor * entries, entries)


def levels(stream_key, dims, cuts, least, top_value):
    def one(position, parts):
        steps = jax.random.uniform(jax.random.fold_in(jax.random.fold_in(stream_key, 6), position), (parts,), jnp.float32, least / len(cuts), top_value / len(cuts))
        return jnp.repeat(jnp.exp(steps), dims[position] // parts).reshape((-1,) + (1,) * (len(dims) - position - 1))

    factor_of = one(*cuts[0])
    for cut in cuts[1:]:
        factor_of = factor_of * one(*cut)
    return factor_of


def normal_values(rng, shape, width, most, pieces=(), kind=jnp.bfloat16):
    values = jax.random.normal(rng, shape, jnp.float32) * width
    if len(pieces) > 0:
        values = levels(rng, shape, pieces, -0.22, 0.18) * values
    return jnp.clip(values, min=-most, max=most).astype(kind)


def gaussian_with(key, extent, width, most, shards, heavy, held_as=jnp.bfloat16):
    values = width * jax.random.normal(key, extent, jnp.float32)
    if shards:
        values = values * levels(key, extent, shards, -0.22, 0.18)
    return jnp.clip(with_spikes(values, jax.random.fold_in(key, 3), *heavy), -most, most).astype(held_as)


def setup_inputs(seed: int = 0) -> dict:
    seeds = jax.random.split(jax.random.key(seed), 13)
    return {
        "hidden": normal_values(seeds[0], (TOKENS, D), 1.0, 6.0, ((0, 32),), jnp.float32),
        "segments": draw_segments(jax.random.fold_in(seeds[12], 71), 0),
        "w_qkv": normal_values(seeds[2], (LAYERS, D, 3 * D), D ** -0.5, 0.21875, ((1, 8), (2, 4))),
        "w_out": normal_values(seeds[3], (LAYERS, D, D), (D // 16) ** -0.5, 0.875, ((1, 8), (2, 4))),
        "w_up": normal_values(seeds[4], (LAYERS, D, FF), D ** -0.5, 0.21875, ((1, 8), (2, 4))),
        "w_down": normal_values(seeds[5], (LAYERS, D, FF), FF ** -0.5, 0.109375, ((1, 8), (2, 4))),
        "ln_gain": jnp.clip(1.0 + 0.1 * jax.random.normal(seeds[6], (LAYERS, 2, D), jnp.float32), 0.5, 1.5),
        "ln_bias": normal_values(seeds[7], (LAYERS, 2, D), 0.3, 1.8, (), jnp.float32),
        "branch_bias": normal_values(seeds[8], (LAYERS, D), 0.3, 1.8, (), jnp.float32),
        "qkv_bias": normal_values(seeds[9], (LAYERS, 3 * D), 0.3, 1.8, (), jnp.float32),
        "up_bias": normal_values(seeds[10], (LAYERS, FF), 0.3, 1.8, (), jnp.float32),
        "cotangent": gaussian_with(seeds[11], (TOKENS, D), 1.0, 6.0, ((0, 32),), (0, 1, 32, 2.75), jnp.float32),
    }


NORM_EPS = 1e-05
MASKED = -1e+30
PRECISE = lax.Precision.HIGHEST

@jax.custom_vjp
def low(v):
    return lax.optimization_barrier(v.astype(jnp.bfloat16)).astype(jnp.float32)

@jax.custom_vjp
def low_back(v):
    return v

def low_keep(v):
    return (low(v), None)

def low_pass(kept, grad):
    return (grad,)

def back_keep(v):
    return (v, None)

def back_low(kept, grad):
    return (low(grad),)
low.defvjp(low_keep, low_pass)
low_back.defvjp(back_keep, back_low)

def layer_norm(values_in, gain, shift):
    average = lax.optimization_barrier(jnp.mean(values_in, axis=-1, keepdims=True))
    centered = values_in - average
    variance = lax.optimization_barrier(jnp.mean(centered * centered, axis=-1, keepdims=True))
    return centered * lax.rsqrt(variance + NORM_EPS) * gain + shift

def positions(seg_group):
    places = jnp.arange(seg_group.shape[0], dtype=jnp.int32)
    fresh = jnp.concatenate([jnp.ones((1,), dtype=bool), seg_group[1:] != seg_group[:-1]])
    starts = lax.cummax(jnp.where(fresh, places, 0).astype(jnp.int32), axis=0)
    return places - starts

def rotary_tables(token_place):
    half_rot = ROT // 2
    exponent = jnp.arange(half_rot, dtype=jnp.float32) * (-2.0 * math.log(10000.0) / ROT)
    angles = token_place.astype(jnp.float32)[:, None] * jnp.exp(exponent)[None, :]
    return (jnp.cos(angles), jnp.sin(angles))

def rotate_heads(heads, cosine, sine_table):
    half_rot = ROT // 2
    first_half = heads[..., :half_rot]
    second_half = heads[..., half_rot:ROT]
    cos_wide = cosine[:, None, :]
    sin_wide = sine_table[:, None, :]
    return jnp.concatenate([first_half * cos_wide - second_half * sin_wide, second_half * cos_wide + first_half * sin_wide, heads[..., ROT:]], axis=-1)

def attend(queries, keys_in, values_in, seg_group):
    places = jnp.arange(seg_group.shape[0], dtype=jnp.int32)
    allowed = (seg_group[:, None] == seg_group[None, :]) & (places[None, :] <= places[:, None])
    scores = low_back(jnp.einsum('qhd,khd->hqk', queries, keys_in, precision=PRECISE) * HEAD_DIM ** (-0.5))
    scores = jnp.where(allowed[None], scores, MASKED)
    row_max = lax.optimization_barrier(jnp.max(scores, axis=-1, keepdims=True))
    exp_scores = jnp.exp(scores - row_max)
    prob_low = low(exp_scores / lax.optimization_barrier(jnp.sum(exp_scores, axis=-1, keepdims=True)))
    return jnp.einsum('hqk,khd->qhd', prob_low, values_in, precision=PRECISE)

def group_view(array_in, groups):
    return array_in.reshape(groups, GROUP_TOK, HEADS, HEAD_DIM)

def forward(hidden, w_qkv, w_out, w_up, w_down, ln_gain, ln_bias, branch_bias, qkv_bias, up_bias, segments):
    token_count = hidden.shape[0]
    groups = token_count // GROUP_TOK
    seg_groups = segments.reshape(groups, GROUP_TOK)
    token_place = jax.vmap(positions)(seg_groups).reshape(token_count)
    cosine, sine_table = rotary_tables(token_place)
    attend_saved = jax.checkpoint(attend)

    def attend_member(member):
        return attend_saved(member[0], member[1], member[2], member[3])
    for which_layer in range(LAYERS):
        normed_one = low(layer_norm(hidden, ln_gain[which_layer, 0], ln_bias[which_layer, 0]))
        normed_two = low(layer_norm(hidden, ln_gain[which_layer, 1], ln_bias[which_layer, 1]))
        mixed_cols = low_back(jnp.dot(normed_one, w_qkv[which_layer], precision=PRECISE) + qkv_bias[which_layer])
        mixed_cols = mixed_cols.reshape(token_count, HEADS, 3, HEAD_DIM)
        queries = low(rotate_heads(mixed_cols[:, :, 0], cosine, sine_table))
        keys_all = low(rotate_heads(mixed_cols[:, :, 1], cosine, sine_table))
        values_all = low(mixed_cols[:, :, 2])
        context = lax.map(attend_member, (group_view(queries, groups), group_view(keys_all, groups), group_view(values_all, groups), seg_groups))
        context = low_back(low(context.reshape(token_count, D)))
        up_proj = low_back(jnp.dot(normed_two, w_up[which_layer], precision=PRECISE) + up_bias[which_layer])
        activated = low(jax.nn.gelu(up_proj, approximate=False))
        branch = jnp.dot(context, w_out[which_layer].T, precision=PRECISE) + jnp.dot(activated, w_down[which_layer].T, precision=PRECISE) + branch_bias[which_layer]
        hidden = hidden + low_back(branch)
    return hidden

def reference(hidden, segments, w_qkv, w_out, w_up, w_down, ln_gain, ln_bias, branch_bias, qkv_bias, up_bias, cotangent):

    def run_layers(hidden_in, qkv_in, out_in, up_in, down_in, gain_in, shift_in, branch_in, qkv_shift, up_shift):
        return forward(hidden_in, qkv_in, out_in, up_in, down_in, gain_in, shift_in, branch_in, qkv_shift, up_shift, segments)
    result, pull_back = jax.vjp(run_layers, hidden.astype(jnp.float32), w_qkv.astype(jnp.float32), w_out.astype(jnp.float32), w_up.astype(jnp.float32), w_down.astype(jnp.float32), ln_gain.astype(jnp.float32), ln_bias.astype(jnp.float32), branch_bias.astype(jnp.float32), qkv_bias.astype(jnp.float32), up_bias.astype(jnp.float32))
    grads = pull_back(cotangent.astype(jnp.float32))
    return (result, grads[0], grads[1], grads[2], grads[3], grads[4], grads[5], grads[6], grads[7], grads[8], grads[9])
```

```python
import math

import jax
import jax.numpy as jnp
from jax import lax
from jax.experimental import pallas as pl
from jax.experimental.pallas import tpu as pltpu
from jax.sharding import PartitionSpec as P

D = 768
HEADS = 12
HEAD_DIM = 64
FF = 3072
ROT = 16
HALF = ROT // 2
LAYERS = 2
NORM_EPS = 1e-05
MASKED = -1e30
SCALE = HEAD_DIM ** (-0.5)
BF = jnp.bfloat16
F32 = jnp.float32


def dot(left, right, left_dim, right_dim):
    return lax.dot_general(
        left, right, (((left_dim,), (right_dim,)), ((), ())), preferred_element_type=F32
    )


def swap(values, axis, bit):
    count = lax.axis_size(axis)
    return lax.ppermute(values, axis, [(i, i ^ (1 << bit)) for i in range(count)])


def gather_rows(block, axis):
    count = lax.axis_size(axis)
    rank = lax.axis_index(axis)
    held = block[None]
    for bit in reversed(range(count.bit_length() - 1)):
        other = swap(held, axis, bit)
        first = ((rank >> bit) & 1) == 0
        held = jnp.stack(
            [jnp.where(first, held, other), jnp.where(first, other, held)], axis=1
        ).reshape((2 * held.shape[0],) + block.shape)
    return held.reshape((count * block.shape[0],) + block.shape[1:])


def scatter_rows(total, axis):
    count = lax.axis_size(axis)
    rank = lax.axis_index(axis)
    rows = total.shape[0] // count
    held = total.reshape((count, rows) + total.shape[1:])
    for bit in range(count.bit_length() - 1):
        mine = (rank >> bit) & 1
        pairs = held.reshape((held.shape[0] // 2, 2) + held.shape[1:])
        keep = lax.dynamic_index_in_dim(pairs, mine, axis=1, keepdims=False)
        send = lax.dynamic_index_in_dim(pairs, 1 - mine, axis=1, keepdims=False)
        held = keep + swap(send.astype(BF), axis, bit).astype(F32)
    return held[0]


def sum_over(values, axis):
    for bit in range(lax.axis_size(axis).bit_length() - 1):
        values = values + swap(values, axis, bit)
    return values


def segment_starts(seg_group):
    places = jnp.arange(seg_group.shape[0], dtype=jnp.int32)
    fresh = jnp.concatenate([jnp.ones((1,), dtype=bool), seg_group[1:] != seg_group[:-1]])
    return lax.cummax(jnp.where(fresh, places, 0), axis=0)


def turned(rows, cosine, sine):
    first, second = rows[:HALF], rows[HALF:ROT]
    return jnp.concatenate(
        [first * cosine - second * sine, second * cosine + first * sine, rows[ROT:]], axis=0
    )


def masked_scores(keys, queries, starts, first_query):
    scores = dot(keys, queries, 0, 0)
    key_place = lax.broadcasted_iota(jnp.int32, scores.shape, 0)
    query_place = lax.broadcasted_iota(jnp.int32, scores.shape, 1) + first_query
    allowed = (key_place <= query_place) & (key_place >= starts)
    return jnp.where(allowed, scores, MASKED)


def forward_kernel(block, mixed_ref, cos_ref, sin_ref, start_ref, qkv_ref, ctx_ref, log_ref):
    cosine, sine = cos_ref[...], sin_ref[...]
    queries = turned(mixed_ref[:HEAD_DIM], cosine, sine).astype(BF)
    keys = turned(mixed_ref[HEAD_DIM : 2 * HEAD_DIM], cosine, sine).astype(BF)
    values = mixed_ref[2 * HEAD_DIM :].astype(BF)
    qkv_ref[:HEAD_DIM] = queries
    qkv_ref[HEAD_DIM : 2 * HEAD_DIM] = keys
    qkv_ref[2 * HEAD_DIM :] = values
    for first in range(0, mixed_ref.shape[1], block):
        here = slice(first, first + block)
        seen = first + block
        scaled = queries[:, here] * jnp.asarray(SCALE, BF)
        scores = masked_scores(keys[:, :seen], scaled, start_ref[:, here], first)
        top = jnp.max(scores, axis=0, keepdims=True)
        weights = jnp.exp(scores - top)
        total = jnp.sum(weights, axis=0, keepdims=True)
        context = dot(values[:, :seen], weights.astype(BF), 1, 0)
        ctx_ref[:, here] = (context / total).astype(BF)
        log_ref[:, here] = jnp.broadcast_to(top + jnp.log(total), (8, block))


def backward_kernel(
    block, qkv_ref, grad_ref, log_ref, cos_ref, sin_ref, start_ref, out_ref, dq_ref, dk_ref, dv_ref
):
    dk_ref[...] = jnp.zeros_like(dk_ref)
    dv_ref[...] = jnp.zeros_like(dv_ref)
    for first in range(0, qkv_ref.shape[1], block):
        here = slice(first, first + block)
        seen = first + block
        scaled = qkv_ref[:HEAD_DIM, here] * jnp.asarray(SCALE, BF)
        keys = qkv_ref[HEAD_DIM : 2 * HEAD_DIM, :seen]
        values = qkv_ref[2 * HEAD_DIM :, :seen]
        grad = grad_ref[:, here]
        scores = masked_scores(keys, scaled, start_ref[:, here], first)
        prob = jnp.exp(scores - log_ref[:1, here])
        grad_prob = dot(values, grad, 0, 0)
        inner = jnp.sum(prob * grad_prob, axis=0, keepdims=True)
        grad_scores = (prob * (grad_prob - inner)).astype(BF)
        dv_ref[:, :seen] += dot(grad, prob.astype(BF), 1, 1)
        dk_ref[:, :seen] += dot(scaled, grad_scores, 1, 1)
        dq_ref[:, here] = dot(keys, grad_scores, 1, 0) * SCALE
    cosine, sine = cos_ref[...], sin_ref[...]
    out_ref[:HEAD_DIM] = turned(dq_ref[...], cosine, -sine).astype(BF)
    out_ref[HEAD_DIM : 2 * HEAD_DIM] = turned(dk_ref[...], cosine, -sine).astype(BF)
    out_ref[2 * HEAD_DIM :] = dv_ref[...].astype(BF)


def by_head(rows, tokens):
    return pl.BlockSpec((rows, tokens), lambda h: (h, 0))


def shared(rows, tokens):
    return pl.BlockSpec((rows, tokens), lambda h: (0, 0))


def attention_forward(mixed, cosine, sine, starts, heads):
    tokens = mixed.shape[1]
    block = min(512, tokens)
    return pl.pallas_call(
        lambda *refs: forward_kernel(block, *refs),
        grid=(heads,),
        in_specs=[
            by_head(3 * HEAD_DIM, tokens),
            shared(HALF, tokens),
            shared(HALF, tokens),
            shared(1, tokens),
        ],
        out_specs=[by_head(3 * HEAD_DIM, tokens), by_head(HEAD_DIM, tokens), by_head(8, tokens)],
        out_shape=[
            jax.ShapeDtypeStruct((heads * 3 * HEAD_DIM, tokens), BF),
            jax.ShapeDtypeStruct((heads * HEAD_DIM, tokens), BF),
            jax.ShapeDtypeStruct((heads * 8, tokens), F32),
        ],
        compiler_params=pltpu.CompilerParams(vmem_limit_bytes=48 * 2**20),
        cost_estimate=pl.CostEstimate(
            flops=10**10, bytes_accessed=8 * 10**6, transcendentals=heads * tokens * tokens
        ),
    )(mixed, cosine, sine, starts)


def attention_backward(qkv, grad_context, logsum, cosine, sine, starts, heads):
    tokens = qkv.shape[1]
    block = min(512, tokens)
    return pl.pallas_call(
        lambda *refs: backward_kernel(block, *refs),
        grid=(heads,),
        in_specs=[
            by_head(3 * HEAD_DIM, tokens),
            by_head(HEAD_DIM, tokens),
            by_head(8, tokens),
            shared(HALF, tokens),
            shared(HALF, tokens),
            shared(1, tokens),
        ],
        out_specs=by_head(3 * HEAD_DIM, tokens),
        out_shape=jax.ShapeDtypeStruct((heads * 3 * HEAD_DIM, tokens), BF),
        scratch_shapes=[pltpu.VMEM((HEAD_DIM, tokens), F32)] * 3,
        compiler_params=pltpu.CompilerParams(vmem_limit_bytes=48 * 2**20),
        cost_estimate=pl.CostEstimate(
            flops=25 * 10**9, bytes_accessed=8 * 10**6, transcendentals=heads * tokens * tokens
        ),
    )(qkv, grad_context, logsum, cosine, sine, starts)


def local(
    hidden,
    segments,
    w_qkv,
    w_out,
    w_up,
    w_down,
    ln_gain,
    ln_bias,
    branch_bias,
    qkv_bias,
    up_bias,
    cotangent,
):
    tensor_rank = lax.axis_index("tensor")
    tensor_count = lax.axis_size("tensor")
    local_heads = HEADS // tensor_count
    width_qkv = w_qkv.shape[2]
    width_up = w_up.shape[2]
    tokens = segments.shape[0]

    starts = segment_starts(segments)
    place = jnp.arange(tokens, dtype=jnp.int32) - starts
    exponent = jnp.arange(HALF, dtype=F32) * (-2.0 * math.log(10000.0) / ROT)
    angles = jnp.exp(exponent)[:, None] * place.astype(F32)[None, :]
    cosine, sine = jnp.cos(angles), jnp.sin(angles)
    starts = starts[None, :]

    weights = []
    for layer in range(LAYERS):
        into = gather_rows(jnp.concatenate([w_up[layer], w_qkv[layer]], axis=1), "dp")
        back = gather_rows(jnp.concatenate([w_down[layer], w_out[layer]], axis=1), "dp")
        weights.append((into[:, width_up:], back[:, width_up:], into[:, :width_up], back[:, :width_up]))

    stored = []
    for layer in range(LAYERS):
        qkv_full, out_full, up_full, down_full = weights[layer]
        average = jnp.mean(hidden, axis=-1, keepdims=True)
        centered = hidden - average
        variance = jnp.mean(centered * centered, axis=-1, keepdims=True)
        root = lax.rsqrt(variance + NORM_EPS)
        unit = centered * root
        unit_rows = gather_rows(unit.astype(BF), "tensor")
        wide = unit_rows.astype(F32)
        rows_one = (wide * ln_gain[layer, 0] + ln_bias[layer, 0]).astype(BF)
        rows_two = (wide * ln_gain[layer, 1] + ln_bias[layer, 1]).astype(BF)
        qkv_here = lax.dynamic_slice_in_dim(qkv_bias[layer], tensor_rank * width_qkv, width_qkv)
        mixed = dot(qkv_full, rows_one, 0, 1) + qkv_here[:, None]
        qkv, context, logsum = attention_forward(mixed, cosine, sine, starts, local_heads)
        up_here = lax.dynamic_slice_in_dim(up_bias[layer], tensor_rank * width_up, width_up)
        up_proj = dot(rows_two, up_full, 1, 0) + up_here
        activated = jax.nn.gelu(up_proj, approximate=False).astype(BF)
        branch = scatter_rows(
            dot(activated, down_full, 1, 1) + dot(context, out_full, 0, 1), "tensor"
        )
        stored.append((unit, root, unit_rows, qkv, context, logsum, up_proj, activated))
        hidden = hidden + branch + branch_bias[layer]

    grad_hidden = cotangent
    weight_parts = [None] * LAYERS
    small_parts = [None] * LAYERS
    inverse_root = 1.0 / math.sqrt(2.0)
    density = 1.0 / math.sqrt(2.0 * math.pi)
    for layer in reversed(range(LAYERS)):
        unit, root, unit_rows, qkv, context, logsum, up_proj, activated = stored[layer]
        qkv_full, out_full, up_full, down_full = weights[layer]
        gain_one, gain_two = ln_gain[layer, 0], ln_gain[layer, 1]
        shift_one, shift_two = ln_bias[layer, 0], ln_bias[layer, 1]
        grad_branch = grad_hidden.astype(BF)
        branch_sum = jnp.sum(grad_branch.astype(F32), axis=0)
        grad_rows = gather_rows(grad_branch, "tensor")

        grad_context = dot(out_full, grad_rows, 0, 1).astype(BF)
        grad_mixed = attention_backward(
            qkv, grad_context, logsum, cosine, sine, starts, local_heads
        )
        grad_act = dot(grad_rows, down_full, 1, 0)
        normal_cdf = 0.5 * (1.0 + lax.erf(up_proj * inverse_root))
        slope = normal_cdf + up_proj * jnp.exp(-0.5 * up_proj * up_proj) * density
        grad_up = (grad_act * slope).astype(BF)

        grad_unit = scatter_rows(
            dot(grad_mixed, qkv_full, 0, 1) * gain_one + dot(grad_up, up_full, 1, 1) * gain_two,
            "tensor",
        )
        pull = grad_unit - jnp.mean(grad_unit, axis=-1, keepdims=True)
        pull = pull - unit * jnp.mean(grad_unit * unit, axis=-1, keepdims=True)
        grad_hidden = grad_hidden + root * pull

        back_grad = jnp.concatenate(
            [dot(grad_rows, activated, 0, 0), dot(grad_rows, context, 0, 1)], axis=1
        )
        up_sum = jnp.sum(grad_up.astype(F32), axis=0)
        qkv_sum = jnp.sum(grad_mixed.astype(F32), axis=1)
        up_unit = dot(unit_rows, grad_up, 0, 0)
        qkv_unit = dot(unit_rows, grad_mixed, 0, 1)
        up_grad = up_unit * gain_two[:, None] + shift_two[:, None] * up_sum
        qkv_grad = qkv_unit * gain_one[:, None] + shift_one[:, None] * qkv_sum
        up_wide, qkv_wide = up_full.astype(F32), qkv_full.astype(F32)
        weight_parts[layer] = (
            scatter_rows(back_grad, "dp"),
            scatter_rows(up_grad, "dp"),
            scatter_rows(qkv_grad, "dp"),
        )
        small = jnp.concatenate(
            [
                jnp.sum(qkv_wide * qkv_unit, axis=1),
                jnp.sum(up_wide * up_unit, axis=1),
                jnp.sum(qkv_wide * qkv_sum, axis=1),
                jnp.sum(up_wide * up_sum, axis=1),
                branch_sum,
                up_sum,
                qkv_sum,
            ]
        )
        small_parts[layer] = gather_rows(sum_over(small, "dp")[None], "tensor")

    small_all = jnp.stack(small_parts)
    summed = jnp.sum(small_all[:, :, : 5 * D], axis=1).reshape(LAYERS, 5, D)
    up_total = small_all[:, :, 5 * D : 5 * D + width_up].reshape(LAYERS, FF)
    qkv_total = small_all[:, :, 5 * D + width_up :].reshape(LAYERS, 3 * D)
    back_all = jnp.stack([parts[0] for parts in weight_parts])
    return (
        hidden,
        grad_hidden,
        jnp.stack([parts[2] for parts in weight_parts]),
        back_all[:, :, width_up:],
        jnp.stack([parts[1] for parts in weight_parts]),
        back_all[:, :, :width_up],
        summed[:, 0:2],
        summed[:, 2:4],
        summed[:, 4],
        qkv_total,
        up_total,
    )


def solution(mesh):
    return jax.shard_map(
        local,
        mesh=mesh,
        in_specs=(
            P(("dp", "tensor"), None),
            P("dp"),
            P(None, "dp", "tensor"),
            P(None, "dp", "tensor"),
            P(None, "dp", "tensor"),
            P(None, "dp", "tensor"),
            P(),
            P(),
            P(),
            P(),
            P(),
            P(("dp", "tensor"), None),
        ),
        out_specs=(
            P(("dp", "tensor"), None),
            P(("dp", "tensor"), None),
            P(None, "dp", "tensor"),
            P(None, "dp", "tensor"),
            P(None, "dp", "tensor"),
            P(None, "dp", "tensor"),
            P(),
            P(),
            P(),
            P(),
            P(),
        ),
        check_vma=False,
    )
```

```python
import math

import jax
import jax.numpy as jnp
from jax import lax
from jax.experimental import pallas as pl
from jax.experimental.pallas import tpu as pltpu
from jax.sharding import PartitionSpec as P

D = 768
HEADS = 12
HEAD_DIM = 64
FF = 3072
ROT = 16
HALF = ROT // 2
LAYERS = 2
NORM_EPS = 1e-05
MASKED = -1e30
SCALE = HEAD_DIM ** (-0.5)
BF = jnp.bfloat16
F32 = jnp.float32


def dot(left, right, left_dim, right_dim):
    return lax.dot_general(
        left, right, (((left_dim,), (right_dim,)), ((), ())), preferred_element_type=F32
    )


def swap(values, axis, bit):
    count = lax.axis_size(axis)
    return lax.ppermute(values, axis, [(i, i ^ (1 << bit)) for i in range(count)])


def after(values, *markers):
    return lax.optimization_barrier((values,) + markers)[0]


def gather_steps(block, axis, turns=None):
    count = lax.axis_size(axis)
    rank = lax.axis_index(axis)
    held = block[None]
    arrived = []
    joined = None
    for bit in reversed(range(count.bit_length() - 1)):
        if joined is not None:
            held = joined()
        way = min(bit, 1)
        if turns is not None and way in turns:
            held = after(held, turns[way])
        other = swap(held, axis, bit)
        if turns is not None:
            turns[way] = other
        arrived.append(other)

        def joined(*markers, held=held, other=other, bit=bit):
            if markers:
                other = after(other, *markers)
            first = ((rank >> bit) & 1) == 0
            return jnp.stack(
                [jnp.where(first, held, other), jnp.where(first, other, held)], axis=1
            ).reshape((2 * held.shape[0],) + block.shape)

    def finish(*markers):
        whole = block[None] if joined is None else joined(*markers)
        return whole.reshape((count * block.shape[0],) + block.shape[1:])

    return finish, arrived


def gather_rows(block, axis):
    return gather_steps(block, axis)[0]()


def scatter_rows(totals, axis, waits=(), arrived=None):
    count = lax.axis_size(axis)
    rank = lax.axis_index(axis)
    held = [total.reshape((count, total.shape[0] // count, total.shape[1])) for total in totals]
    for bit in range(count.bit_length() - 1):
        mine = (rank >> bit) & 1
        pairs = [part.reshape((part.shape[0] // 2, 2) + part.shape[1:]) for part in held]
        keep = [lax.dynamic_index_in_dim(part, mine, axis=1, keepdims=False) for part in pairs]
        send = [
            lax.dynamic_index_in_dim(part, 1 - mine, axis=1, keepdims=False).astype(BF)
            for part in pairs
        ]
        other = swap(send[0] if len(send) == 1 else jnp.concatenate(send, axis=2), axis, bit)
        if arrived is not None:
            arrived.append(other)
        if bit < len(waits):
            other = after(other, waits[bit])
        held, begin = [], 0
        for part in keep:
            end = begin + part.shape[2]
            held.append(part + other[:, :, begin:end].astype(F32))
            begin = end
    return [part[0] for part in held]


def sum_over(values, axis):
    for bit in range(lax.axis_size(axis).bit_length() - 1):
        values = values + swap(values, axis, bit)
    return values


def segment_starts(seg_group):
    places = jnp.arange(seg_group.shape[0], dtype=jnp.int32)
    fresh = jnp.concatenate([jnp.ones((1,), dtype=bool), seg_group[1:] != seg_group[:-1]])
    return lax.cummax(jnp.where(fresh, places, 0), axis=0)


def turned(rows, cosine, sine):
    first, second = rows[:HALF], rows[HALF:ROT]
    return jnp.concatenate(
        [first * cosine - second * sine, second * cosine + first * sine, rows[ROT:]], axis=0
    )


def masked_scores(keys, queries, starts, first_query):
    scores = dot(keys, queries, 0, 0)
    key_place = lax.broadcasted_iota(jnp.int32, scores.shape, 0)
    query_place = lax.broadcasted_iota(jnp.int32, scores.shape, 1) + first_query
    allowed = (key_place <= query_place) & (key_place >= starts)
    return jnp.where(allowed, scores, MASKED)


def forward_kernel(block, mixed_ref, cos_ref, sin_ref, start_ref, qkv_ref, ctx_ref, log_ref):
    cosine, sine = cos_ref[...], sin_ref[...]
    queries = turned(mixed_ref[:HEAD_DIM], cosine, sine).astype(BF)
    keys = turned(mixed_ref[HEAD_DIM : 2 * HEAD_DIM], cosine, sine).astype(BF)
    values = mixed_ref[2 * HEAD_DIM :].astype(BF)
    qkv_ref[:HEAD_DIM] = queries
    qkv_ref[HEAD_DIM : 2 * HEAD_DIM] = keys
    qkv_ref[2 * HEAD_DIM :] = values
    for first in range(0, mixed_ref.shape[1], block):
        here = slice(first, first + block)
        seen = first + block
        scaled = queries[:, here] * jnp.asarray(SCALE, BF)
        scores = masked_scores(keys[:, :seen], scaled, start_ref[:, here], first)
        top = jnp.max(scores, axis=0, keepdims=True)
        weights = jnp.exp(scores - top)
        total = jnp.sum(weights, axis=0, keepdims=True)
        context = dot(values[:, :seen], weights.astype(BF), 1, 0)
        ctx_ref[:, here] = (context / total).astype(BF)
        log_ref[:, here] = jnp.broadcast_to(top + jnp.log(total), (8, block))


def backward_kernel(
    block, qkv_ref, grad_ref, log_ref, cos_ref, sin_ref, start_ref, out_ref, dq_ref, dk_ref, dv_ref
):
    dk_ref[...] = jnp.zeros_like(dk_ref)
    dv_ref[...] = jnp.zeros_like(dv_ref)
    for first in range(0, qkv_ref.shape[1], block):
        here = slice(first, first + block)
        seen = first + block
        scaled = qkv_ref[:HEAD_DIM, here] * jnp.asarray(SCALE, BF)
        keys = qkv_ref[HEAD_DIM : 2 * HEAD_DIM, :seen]
        values = qkv_ref[2 * HEAD_DIM :, :seen]
        grad = grad_ref[:, here]
        scores = masked_scores(keys, scaled, start_ref[:, here], first)
        prob = jnp.exp(scores - log_ref[:1, here])
        grad_prob = dot(values, grad, 0, 0)
        inner = jnp.sum(prob * grad_prob, axis=0, keepdims=True)
        grad_scores = (prob * (grad_prob - inner)).astype(BF)
        dv_ref[:, :seen] += dot(grad, prob.astype(BF), 1, 1)
        dk_ref[:, :seen] += dot(scaled, grad_scores, 1, 1)
        dq_ref[:, here] = dot(keys, grad_scores, 1, 0) * SCALE
    cosine, sine = cos_ref[...], sin_ref[...]
    out_ref[:HEAD_DIM] = turned(dq_ref[...], cosine, -sine).astype(BF)
    out_ref[HEAD_DIM : 2 * HEAD_DIM] = turned(dk_ref[...], cosine, -sine).astype(BF)
    out_ref[2 * HEAD_DIM :] = dv_ref[...].astype(BF)


def by_head(rows, tokens):
    return pl.BlockSpec((rows, tokens), lambda h: (h, 0))


def shared(rows, tokens):
    return pl.BlockSpec((rows, tokens), lambda h: (0, 0))


def attention_forward(mixed, cosine, sine, starts, heads):
    tokens = mixed.shape[1]
    block = min(512, tokens)
    return pl.pallas_call(
        lambda *refs: forward_kernel(block, *refs),
        grid=(heads,),
        in_specs=[
            by_head(3 * HEAD_DIM, tokens),
            shared(HALF, tokens),
            shared(HALF, tokens),
            shared(1, tokens),
        ],
        out_specs=[by_head(3 * HEAD_DIM, tokens), by_head(HEAD_DIM, tokens), by_head(8, tokens)],
        out_shape=[
            jax.ShapeDtypeStruct((heads * 3 * HEAD_DIM, tokens), BF),
            jax.ShapeDtypeStruct((heads * HEAD_DIM, tokens), BF),
            jax.ShapeDtypeStruct((heads * 8, tokens), F32),
        ],
        compiler_params=pltpu.CompilerParams(vmem_limit_bytes=48 * 2**20),
        cost_estimate=pl.CostEstimate(
            flops=10**10, bytes_accessed=8 * 10**6, transcendentals=heads * tokens * tokens
        ),
    )(mixed, cosine, sine, starts)


def attention_backward(qkv, grad_context, logsum, cosine, sine, starts, heads):
    tokens = qkv.shape[1]
    block = min(512, tokens)
    return pl.pallas_call(
        lambda *refs: backward_kernel(block, *refs),
        grid=(heads,),
        in_specs=[
            by_head(3 * HEAD_DIM, tokens),
            by_head(HEAD_DIM, tokens),
            by_head(8, tokens),
            shared(HALF, tokens),
            shared(HALF, tokens),
            shared(1, tokens),
        ],
        out_specs=by_head(3 * HEAD_DIM, tokens),
        out_shape=jax.ShapeDtypeStruct((heads * 3 * HEAD_DIM, tokens), BF),
        scratch_shapes=[pltpu.VMEM((HEAD_DIM, tokens), F32)] * 3,
        compiler_params=pltpu.CompilerParams(vmem_limit_bytes=48 * 2**20),
        cost_estimate=pl.CostEstimate(
            flops=25 * 10**9, bytes_accessed=8 * 10**6, transcendentals=heads * tokens * tokens
        ),
    )(qkv, grad_context, logsum, cosine, sine, starts)


def local(
    hidden,
    segments,
    w_qkv,
    w_out,
    w_up,
    w_down,
    ln_gain,
    ln_bias,
    branch_bias,
    qkv_bias,
    up_bias,
    cotangent,
):
    tensor_rank = lax.axis_index("tensor")
    tensor_count = lax.axis_size("tensor")
    local_heads = HEADS // tensor_count
    width_qkv = w_qkv.shape[2]
    width_up = w_up.shape[2]
    tokens = segments.shape[0]

    starts = segment_starts(segments)
    place = jnp.arange(tokens, dtype=jnp.int32) - starts
    exponent = jnp.arange(HALF, dtype=F32) * (-2.0 * math.log(10000.0) / ROT)
    angles = jnp.exp(exponent)[:, None] * place.astype(F32)[None, :]
    cosine, sine = jnp.cos(angles), jnp.sin(angles)
    starts = starts[None, :]

    weights = []
    steps = []
    turns = {}
    for layer in range(LAYERS):
        into = gather_steps(jnp.concatenate([w_up[layer], w_qkv[layer]], axis=1), "dp", turns)
        back = gather_steps(jnp.concatenate([w_down[layer], w_out[layer]], axis=1), "dp", turns)
        steps.append((into, back))

    stored = []
    inverse_root = 1.0 / math.sqrt(2.0)
    density = 1.0 / math.sqrt(2.0 * math.pi)
    for layer in range(LAYERS):
        (into_end, into_arrived), (back_end, back_arrived) = steps[layer]
        coming = steps[layer + 1][0][1] if layer + 1 < LAYERS else []
        into = into_end()
        up_full, qkv_full = into[:, :width_up], into[:, width_up:]
        average = jnp.mean(hidden, axis=-1, keepdims=True)
        centered = hidden - average
        variance = jnp.mean(centered * centered, axis=-1, keepdims=True)
        root = lax.rsqrt(variance + NORM_EPS)
        unit = centered * root
        unit_rows = gather_rows(unit.astype(BF), "tensor")
        wide = unit_rows.astype(F32)
        rows_one = (wide * ln_gain[layer, 0] + ln_bias[layer, 0]).astype(BF)
        rows_two = (wide * ln_gain[layer, 1] + ln_bias[layer, 1]).astype(BF)
        qkv_here = lax.dynamic_slice_in_dim(qkv_bias[layer], tensor_rank * width_qkv, width_qkv)
        mixed = dot(qkv_full, rows_one, 0, 1) + qkv_here[:, None]
        if coming:
            mixed = after(mixed, coming[0])
        qkv, context, logsum = attention_forward(mixed, cosine, sine, starts, local_heads)
        up_here = lax.dynamic_slice_in_dim(up_bias[layer], tensor_rank * width_up, width_up)
        up_proj = dot(rows_two, up_full, 1, 0) + up_here
        up_proj, normal_cdf = lax.optimization_barrier(
            (up_proj, 0.5 * (1.0 + lax.erf(up_proj * inverse_root)))
        )
        activated = (up_proj * normal_cdf).astype(BF)
        back = back_end(context)
        down_full, out_full = back[:, :width_up], back[:, width_up:]
        weights.append((qkv_full, out_full, up_full, down_full))
        if len(coming) > 1:
            context = after(context, coming[1])
        arrived = []
        (branch,) = scatter_rows(
            [dot(activated, down_full, 1, 1) + dot(context, out_full, 0, 1)],
            "tensor",
            arrived=arrived,
        )
        stored.append((unit, root, unit_rows, qkv, context, logsum, up_proj, normal_cdf, activated))
        hidden = hidden + branch + branch_bias[layer]

    grad_hidden = cotangent
    weight_parts = [None] * LAYERS
    small_parts = [None] * LAYERS
    waiting = None
    for layer in reversed(range(LAYERS)):
        unit, root, unit_rows, qkv, context, logsum, up_proj, normal_cdf, activated = stored[layer]
        qkv_full, out_full, up_full, down_full = weights[layer]
        gain_one, gain_two = ln_gain[layer, 0], ln_gain[layer, 1]
        shift_one, shift_two = ln_bias[layer, 0], ln_bias[layer, 1]
        grad_branch = grad_hidden.astype(BF)
        branch_sum = jnp.sum(grad_branch.astype(F32), axis=0)
        grad_rows = gather_rows(grad_branch, "tensor")

        def back_grads(rows):
            return [dot(rows, activated, 0, 0), dot(rows, context, 0, 1)]

        def up_grads(pulled):
            total = jnp.sum(pulled.astype(F32), axis=0)
            product = dot(unit_rows, pulled, 0, 0)
            return total, product, product * gain_two[:, None] + shift_two[:, None] * total

        if layer == LAYERS - 1 and arrived:
            grad_rows = after(grad_rows, arrived[0])
        back_grad = back_grads(grad_rows)
        grad_context = dot(out_full, grad_rows, 0, 1).astype(BF)
        grad_act = dot(grad_rows, down_full, 1, 0)
        slope = normal_cdf + up_proj * jnp.exp(-0.5 * up_proj * up_proj) * density
        grad_up = (grad_act * slope).astype(BF)
        if layer == 0:
            up_sum, up_unit, up_grad = up_grads(grad_up)
            grad_context = after(grad_context, up_grad, *back_grad)
        else:
            grad_context = after(grad_context, *back_grad)
        received = []
        if waiting is not None:
            weight_parts[layer + 1], received = waiting(grad_rows, grad_context)
        if received:
            grad_context = after(grad_context, *received[0])
        grad_mixed = attention_backward(
            qkv, grad_context, logsum, cosine, sine, starts, local_heads
        )
        if len(received) > 1:
            grad_up = after(grad_up, *received[1])
        if layer == LAYERS - 1 and len(arrived) > 1:
            grad_up = after(grad_up, arrived[-1])
        unit_part = (
            dot(grad_mixed, qkv_full, 0, 1) * gain_one + dot(grad_up, up_full, 1, 1) * gain_two
        )
        if layer > 0:
            up_sum, up_unit, up_grad = up_grads(after(grad_up, unit_part))
            late_mixed = after(grad_mixed, unit_part)
        else:
            late_mixed = grad_mixed
        (grad_unit,) = scatter_rows([unit_part], "tensor")
        pull = grad_unit - jnp.mean(grad_unit, axis=-1, keepdims=True)
        pull = pull - unit * jnp.mean(grad_unit * unit, axis=-1, keepdims=True)
        grad_hidden = grad_hidden + root * pull

        qkv_sum = jnp.sum(late_mixed.astype(F32), axis=1)
        qkv_unit = dot(unit_rows, late_mixed, 0, 1)
        qkv_grad = qkv_unit * gain_one[:, None] + shift_one[:, None] * qkv_sum

        def sent(
            *markers, back_grad=back_grad, up_grad=up_grad, qkv_grad=qkv_grad, unit_part=unit_part
        ):
            early = (unit_part,) + markers if markers else ()
            up_arrived, qkv_arrived = [], []
            parts = (
                scatter_rows(back_grad, "dp", early)
                + scatter_rows([up_grad], "dp", markers, up_arrived)
                + scatter_rows([qkv_grad], "dp", markers, qkv_arrived)
            )
            return parts, list(zip(up_arrived, qkv_arrived))

        if layer > 0:
            waiting = sent
        else:
            weight_parts[layer] = sent()[0]
        up_wide, qkv_wide = up_full.astype(F32), qkv_full.astype(F32)
        small_parts[layer] = jnp.concatenate(
            [
                jnp.sum(qkv_wide * qkv_unit, axis=1),
                jnp.sum(up_wide * up_unit, axis=1),
                jnp.sum(qkv_wide * qkv_sum, axis=1),
                jnp.sum(up_wide * up_sum, axis=1),
                branch_sum,
                up_sum,
                qkv_sum,
            ]
        )

    small_all = gather_rows(sum_over(jnp.concatenate(small_parts), "dp")[None], "tensor")
    small_all = small_all.reshape(tensor_count, LAYERS, -1).transpose(1, 0, 2)
    summed = jnp.sum(small_all[:, :, : 5 * D], axis=1).reshape(LAYERS, 5, D)
    up_total = small_all[:, :, 5 * D : 5 * D + width_up].reshape(LAYERS, FF)
    qkv_total = small_all[:, :, 5 * D + width_up :].reshape(LAYERS, 3 * D)
    return (
        hidden,
        grad_hidden,
        jnp.stack([parts[3] for parts in weight_parts]),
        jnp.stack([parts[1] for parts in weight_parts]),
        jnp.stack([parts[2] for parts in weight_parts]),
        jnp.stack([parts[0] for parts in weight_parts]),
        summed[:, 0:2],
        summed[:, 2:4],
        summed[:, 4],
        qkv_total,
        up_total,
    )


def solution(mesh):
    return jax.shard_map(
        local,
        mesh=mesh,
        in_specs=(
            P(("dp", "tensor"), None),
            P("dp"),
            P(None, "dp", "tensor"),
            P(None, "dp", "tensor"),
            P(None, "dp", "tensor"),
            P(None, "dp", "tensor"),
            P(),
            P(),
            P(),
            P(),
            P(),
            P(("dp", "tensor"), None),
        ),
        out_specs=(
            P(("dp", "tensor"), None),
            P(("dp", "tensor"), None),
            P(None, "dp", "tensor"),
            P(None, "dp", "tensor"),
            P(None, "dp", "tensor"),
            P(None, "dp", "tensor"),
            P(),
            P(),
            P(),
            P(),
            P(),
        ),
        check_vma=False,
    )
```
